32 devices in a mesh: row: 8 (over y, x, core), col: 4 (over z).
Axes of the slice: x: 2, y: 2, z: 4, core: 2. Of those that a mesh axis runs over, the one named last changes fastest.
Arguments:
- subgrid_pixels: float32 [4096, 2, 2, 1024], P(('row', 'col')), may hold values from -6 to 6
- tile_offsets: int32 [4096, 2], P(('row', 'col')), may hold values from 0 to 255, as said below
- station_pairs: int32 [4096, 2], P(('row', 'col')), may hold values from 0 to 511
- time_blocks: int32 [4096], P(('row', 'col')), may hold values from 0 to 1
- channel_blocks: int32 [4096], P(('row', 'col')), may hold values from 0 to 7
- valid_counts: int32 [32], P(('row', 'col')), may hold values from 64 to 128, as said below
- aterms: bfloat16 [512, 2, 2, 2, 1024], replicated, may hold values from -4 to 4
- channel_weights: float32 [8], replicated, may hold values from 0.5 to 2
Outputs:
- image: float32 [2, 8192, 8192], P(None, ('row', 'col'))
The draws below stay inside these ranges and needn't reach their ends.
Inputs may be any that keep to these rules, and one draw needn't show every extreme that they name: `tile_offsets`: within the valid entries of one device's list, at most 8 subgrids lie in the grid block of any one device (rows 1024 r to 1024 (r + 1) - 1, columns 2048 c to 2048 (c + 1) - 1 of device index r * 4 + c), and some device's block receives exactly 8 valid subgrids from every device. `valid_counts`: entry d counts the valid subgrids of device d, which are the first slots of its list; some device's list is full.
All inputs are finite; a program needn't handle non-finite values.
Results may differ from the reference program's by a relative error of at most 0.0003.
Values sent between devices are 32-bit elements; how exact they have to be, the bound alone decides.
No kernel may reach another device: no remote copies, remote signals or barrier semaphores. Data moves between devices by JAX's collectives and lax.ppermute only.
A program may use at most 320 MiB of HBM per device.

```python
import math
import jax
import jax.numpy as jnp
from jax import lax

G = 8192
SUB = 32
STATIONS = 512
TIME_BLOCKS = 2
CHAN_BLOCKS = 8
SG_DEV = 128
ROWS_DEV = 1024
COLS_DEV = 2048
CAP = 8
SUBGRIDS = 4096
N_ROW = 8
N_COL = 4
DEVICES = 32


def draw_tile_offsets(key, part):
    key = jax.random.fold_in(key, 31)
    hot_key, device_keys, place_key = jax.random.split(key, 3)
    owners = jnp.arange(DEVICES, dtype=jnp.int32)
    owner_row = owners // N_COL
    owner_col = owners % N_COL
    row_offset = (2 * owner_row - (N_ROW - 1)) * (ROWS_DEV // SUB)
    column_offset = (2 * owner_col - (N_COL - 1)) * (COLS_DEV // SUB)
    distance = row_offset * row_offset + column_offset * column_offset
    hot_ranking = (distance * 16 + jax.random.randint(hot_key, (DEVICES,), 0, 16)) * DEVICES + owners
    hottest = jnp.argsort(hot_ranking)[0].astype(jnp.int32)

    def device_plan(device_key):
        first_key, second_key = jax.random.split(device_key)
        jitter = jax.random.randint(first_key, (DEVICES,), 0, jnp.max(distance) + 1)
        ranking = (distance + jitter) * DEVICES + owners
        ranking = jnp.where(owners == hottest, 2 ** 30, ranking)
        ordering = jnp.argsort(ranking).astype(jnp.int32)
        remainder = ordering[jnp.arange(SG_DEV - CAP, dtype=jnp.int32) // CAP]
        remainder = jax.random.permutation(second_key, remainder)
        return jnp.concatenate([jnp.full((CAP,), hottest, jnp.int32), remainder])
    owner_of = jax.vmap(device_plan)(jax.random.split(device_keys, DEVICES))
    row_key, column_key = jax.random.split(place_key)
    row_within = jax.random.randint(row_key, (DEVICES, SG_DEV), 0, ROWS_DEV // SUB)
    column_within = jax.random.randint(column_key, (DEVICES, SG_DEV), 0, COLS_DEV // SUB)
    tile_row = owner_of // N_COL * (ROWS_DEV // SUB) + row_within
    tile_column = owner_of % N_COL * (COLS_DEV // SUB) + column_within
    return jnp.stack([tile_row, tile_column], axis=-1).reshape(DEVICES * SG_DEV, 2).astype(jnp.int32)


def draw_valid_counts(key, part):
    key = jax.random.fold_in(key, 37)
    first_key, second_key = jax.random.split(key)
    counted = jax.random.randint(first_key, (DEVICES,), SG_DEV // 2, SG_DEV + 1)
    full_device = jax.random.randint(second_key, (), 0, DEVICES)
    return jnp.where(jnp.arange(DEVICES) == full_device, SG_DEV, counted).astype(jnp.int32)


def place_ends(entries, stream_key, smallest, top_value):
    longest = entries.shape.index(max(entries.shape))
    spots = []
    for shift in (0, 1):
        where = [jax.random.randint(jax.random.fold_in(stream_key, axis), (), 0, length) for axis, length in enumerate(entries.shape)]
        where[longest] = (where[longest] + shift) % entries.shape[longest]
        spots.append(tuple(where))
    return entries.at[spots[0]].set(smallest).at[spots[1]].set(top_value)


def shard_levels(own_key, shape, pieces, low, largest):
    level = 1.0
    for dim, shards_of in pieces:
        draws = jax.random.uniform(jax.random.fold_in(jax.random.fold_in(own_key, 6), dim), (shards_of,), jnp.float32, low / len(pieces), largest / len(pieces))
        level = level * jnp.repeat(jnp.exp(draws), shape[dim] // shards_of).reshape((-1,) + (1,) * (len(shape) - 1 - dim))
    return level


def centred(rng, shape, spread, bound, pieces=(), kind=jnp.bfloat16):
    entries = jax.random.normal(rng, shape, jnp.float32) * spread
    if len(pieces) > 0:
        entries = shard_levels(rng, shape, pieces, -0.22, 0.18) * entries
    return jnp.clip(entries, min=-bound, max=bound).astype(kind)


def setup_inputs(seed: int = 0) -> dict:
    keys = jax.random.split(jax.random.key(seed), 9)
    subgrid_pixels = centred(keys[0], (SUBGRIDS, 2, 2, SUB * SUB), 1.0, 6.0, ((0, 32),), jnp.float32)
    tile_offsets = draw_tile_offsets(jax.random.fold_in(keys[8], 71), 0)
    station_pairs = place_ends(jax.random.randint(keys[2], (SUBGRIDS, 2), 0, STATIONS), jax.random.fold_in(keys[2], 1), 0, STATIONS - 1).astype(jnp.int32)
    time_blocks = place_ends(jax.random.randint(keys[3], (SUBGRIDS,), 0, TIME_BLOCKS), jax.random.fold_in(keys[3], 1), 0, TIME_BLOCKS - 1).astype(jnp.int32)
    channel_blocks = place_ends(jax.random.randint(keys[4], (SUBGRIDS,), 0, CHAN_BLOCKS), jax.random.fold_in(keys[4], 1), 0, CHAN_BLOCKS - 1).astype(jnp.int32)
    valid_counts = draw_valid_counts(jax.random.fold_in(keys[8], 71), 0)
    aterms = centred(keys[6], (STATIONS, TIME_BLOCKS, 2, 2, SUB * SUB), 0.7, 4.0)
    channel_weights = jnp.clip(jnp.exp(jax.random.uniform(keys[7], (CHAN_BLOCKS,), jnp.float32, math.log(0.5), math.log(2.0))), 0.5, 2.0)
    return {"subgrid_pixels": subgrid_pixels, "tile_offsets": tile_offsets, "station_pairs": station_pairs, "time_blocks": time_blocks, "channel_blocks": channel_blocks, "valid_counts": valid_counts, "aterms": aterms, "channel_weights": channel_weights}


def reference(subgrid_pixels, tile_offsets, station_pairs, time_blocks, channel_blocks, valid_counts, aterms, channel_weights):
    subgrid_total = subgrid_pixels.shape[0]
    slot_index = jnp.arange(subgrid_total, dtype=jnp.int32)
    is_valid = slot_index % SG_DEV < valid_counts[slot_index // SG_DEV]
    beam_first = aterms[station_pairs[:, 0], time_blocks].astype(jnp.float32)
    beam_second = aterms[station_pairs[:, 1], time_blocks].astype(jnp.float32)
    gain_real = beam_first[:, 0] * beam_second[:, 0] + beam_first[:, 1] * beam_second[:, 1]
    gain_imag = beam_first[:, 1] * beam_second[:, 0] - beam_first[:, 0] * beam_second[:, 1]
    weight = (channel_weights[channel_blocks] * is_valid.astype(jnp.float32))[:, None, None]
    pixel_real = subgrid_pixels[:, 0]
    pixel_imag = subgrid_pixels[:, 1]
    fixed_real = (pixel_real * gain_real - pixel_imag * gain_imag) * weight
    fixed_imag = (pixel_real * gain_imag + pixel_imag * gain_real) * weight
    image_field = lax.complex(fixed_real, fixed_imag).reshape(subgrid_total, 2, SUB, SUB)
    spectrum = jnp.fft.fft2(image_field, axes=(2, 3)).reshape(subgrid_total, 2, SUB * SUB) / SUB
    tile_count = G // SUB
    tile_index = tile_offsets[:, 0] * tile_count + tile_offsets[:, 1]
    image_scale = 1.0 / (SUB * math.sqrt(SUBGRIDS))
    images = []
    for feed_index in range(2):
        planes = []
        for component in (jnp.real(spectrum[:, feed_index]), jnp.imag(spectrum[:, feed_index])):
            summed = jax.ops.segment_sum(component, tile_index, num_segments=tile_count * tile_count)
            planes.append(summed.reshape(tile_count, tile_count, SUB, SUB).transpose(0, 2, 1, 3).reshape(G, G))
        transformed = jnp.fft.fft2(lax.complex(planes[0], planes[1]))
        images.append(jnp.real(transformed).T * image_scale)
    return jnp.stack(images).astype(jnp.float32)
```

```python
import math

import jax
import jax.numpy as jnp
import numpy as np
from jax import lax
from jax.experimental import pallas as pl
from jax.experimental.pallas import tpu as pltpu
from jax.sharding import PartitionSpec as P

G = 8192
SUB = 32
TILES = G // SUB
HALF = 2 * SUB
AXES = ("row", "col")
GROUP = 8
IN_FLIGHT = 4
VMEM_LIMIT = 60 * 1024 * 1024


def split(value):
    high = lax.reduce_precision(value, 8, 7)
    return high.astype(jnp.bfloat16), (value - high).astype(jnp.bfloat16)


def subgrid_table():
    index = np.arange(SUB)
    turns = (
        index[:, None, None, None] * index[None, None, :, None]
        + index[None, :, None, None] * index[None, None, None, :]
    ) % SUB
    wave = np.exp(-2j * np.pi / SUB * turns) / SUB
    table = np.zeros((2, SUB, SUB, SUB, 2, SUB))
    table[0, :, :, :, 0, :] = wave.real
    table[0, :, :, :, 1, :] = wave.imag
    table[1, :, :, :, 0, :] = -wave.imag
    table[1, :, :, :, 1, :] = wave.real
    table = table.reshape(2 * SUB * SUB, 2 * SUB * SUB).astype(np.float32)
    high = table.astype(jnp.bfloat16)
    low = (table - high.astype(np.float32)).astype(jnp.bfloat16)
    return high, low


def spectra_of(pixels, pairs, times, channels, valid, aterms, weights):
    slots = pixels.shape[0]
    first = aterms[pairs[:, 0], times].astype(jnp.float32)
    second = aterms[pairs[:, 1], times].astype(jnp.float32)
    gain_real = first[:, 0] * second[:, 0] + first[:, 1] * second[:, 1]
    gain_imag = first[:, 1] * second[:, 0] - first[:, 0] * second[:, 1]
    matches = channels[:, None] == jnp.arange(weights.shape[0], dtype=jnp.int32)[None, :]
    weight = jnp.sum(jnp.where(matches, weights[None, :], 0.0), axis=1)
    weight = jnp.where(valid, weight, 0.0)[:, None, None]
    real = (pixels[:, 0] * gain_real - pixels[:, 1] * gain_imag) * weight
    imag = (pixels[:, 0] * gain_imag + pixels[:, 1] * gain_real) * weight
    fixed = jnp.stack([real, imag], axis=2).reshape(slots * 2, 2 * SUB * SUB)
    table_high, table_low = subgrid_table()
    high, low = split(fixed)
    dot = lambda left, right: jnp.dot(left, right, preferred_element_type=jnp.float32)
    out = dot(high, table_high) + dot(low, table_high) + dot(high, table_low)
    return out.reshape(slots, 2 * SUB // 2, 128)


def phases(turns, modulus):
    angle = (2.0 * math.pi / modulus) * (turns % modulus).astype(jnp.float32)
    return jnp.cos(angle), jnp.sin(angle)


def column_tables(first_m, lanes):
    m = first_m + jnp.arange(lanes, dtype=jnp.int32)
    cos, sin = phases(jnp.arange(SUB, dtype=jnp.int32)[:, None] * m[None, :], G)
    table = jnp.concatenate(
        [jnp.concatenate([cos, -sin], axis=1), jnp.concatenate([sin, cos], axis=1)], axis=0
    )
    high, low = split(table)
    table = jnp.concatenate([high, high, low, jnp.zeros_like(high)], axis=0)
    cos, sin = phases(jnp.arange(TILES, dtype=jnp.int32)[:, None] * m[None, :], TILES)
    turn = jnp.concatenate([cos, -sin], axis=1)
    return table, jnp.broadcast_to(turn[:, None, :], (TILES, 8, 2 * lanes))


def row_table():
    b = jnp.arange(TILES, dtype=jnp.int32)
    u = jnp.arange(SUB, dtype=jnp.int32)
    cos_r, sin_r = phases(b[:, None] * b[None, :], TILES)
    u = u % (SUB // 2) * 2 + u // (SUB // 2)
    cos_u, sin_u = phases(u[:, None] * b[None, :], G)
    cos = cos_r[None] * cos_u[:, :, None] - sin_r[None] * sin_u[:, :, None]
    sin = sin_r[None] * cos_u[:, :, None] + cos_r[None] * sin_u[:, :, None]
    high, low = split(jnp.concatenate([-sin, cos, sin], axis=2))
    return jnp.stack([high, low], axis=1)


def gather_kernel(
    codes, counts, slot_start, x_ref, table_ref, turn_ref, held_ref, out_ref, total, mid, sem, *, first, lanes
):
    step = pl.program_id(0)

    @pl.when(step == 0)
    def _():
        if first:
            total[...] = jnp.zeros_like(total)
        else:
            copy = pltpu.make_async_copy(held_ref, total, sem)
            copy.start()
            copy.wait()

    per_step = x_ref.shape[0]
    is_low = lax.broadcasted_iota(jnp.int32, (GROUP * SUB, 128), 1) < HALF
    for group in range(per_step // GROUP):
        start = group * GROUP

        @pl.when(slot_start + start < counts[step])
        def _():
            x = x_ref[start : start + GROUP].reshape(GROUP * SUB, 128)
            high = x.astype(jnp.bfloat16).astype(jnp.float32)
            low = x - high
            high_turned = pltpu.roll(high, HALF, 1)
            low_turned = pltpu.roll(low, HALF, 1)
            sides = (
                (jnp.where(is_low, high, low_turned), high),
                (jnp.where(is_low, high_turned, low), high_turned),
            )
            for parity, (mixed, other) in enumerate(sides):
                left = jnp.concatenate(
                    [mixed.astype(jnp.bfloat16), other.astype(jnp.bfloat16)], axis=1
                )
                mid[parity] = jnp.dot(left, table_ref[...], preferred_element_type=jnp.float32)
            for item in range(GROUP):
                code = codes[step * per_step + start + item]
                row = code // TILES
                column = code % TILES
                for tile in range(lanes // 128):
                    here = slice(tile * 128, (tile + 1) * 128)
                    there = slice(lanes + tile * 128, lanes + (tile + 1) * 128)
                    turn_real = turn_ref[column, :, here][None]
                    turn_imag = turn_ref[column, :, there][None]
                    for parity in range(2):
                        piece = slice(item * SUB, (item + 1) * SUB)
                        real = mid[parity, piece, here].reshape(SUB // 8, 8, 128)
                        imag = mid[parity, piece, there].reshape(SUB // 8, 8, 128)
                        rows = slice(parity * SUB, (parity + 1) * SUB)
                        total[row, tile, rows] += (real * turn_real - imag * turn_imag).reshape(
                            SUB, 128
                        )
                        total[row, lanes // 128 + tile, rows] += (
                            real * turn_imag + imag * turn_real
                        ).reshape(SUB, 128)

    @pl.when(step == pl.num_programs(0) - 1)
    def _():
        copy = pltpu.make_async_copy(total, out_ref, sem)
        copy.start()
        copy.wait()


def add_columns(chunk, codes, counts, slot_start, table, turn, held, lanes):
    sources = counts.shape[0]
    per_source = chunk.shape[0] // sources
    shape = (TILES, 2 * lanes // 128, 2 * SUB, 128)
    first = held is None
    if first:
        held = jnp.zeros((8, 128), jnp.float32)

    def kernel(*refs):
        gather_kernel(refs[0], refs[1], slot_start, *refs[2:], first=first, lanes=lanes)

    return pl.pallas_call(
        kernel,
        out_shape=jax.ShapeDtypeStruct(shape, jnp.float32),
        grid_spec=pltpu.PrefetchScalarGridSpec(
            num_scalar_prefetch=2,
            grid=(sources,),
            in_specs=[
                pl.BlockSpec((per_source, SUB, 128), lambda i, *_: (i, 0, 0)),
                pl.BlockSpec(table.shape, lambda i, *_: (0, 0)),
                pl.BlockSpec(turn.shape, lambda i, *_: (0, 0, 0)),
                pl.BlockSpec(memory_space=pl.ANY),
            ],
            out_specs=pl.BlockSpec(memory_space=pl.ANY),
            scratch_shapes=[
                pltpu.VMEM(shape, jnp.float32),
                pltpu.VMEM((2, GROUP * SUB, 2 * lanes), jnp.float32),
                pltpu.SemaphoreType.DMA,
            ],
        ),
        input_output_aliases={} if first else {5: 0},
        compiler_params=pltpu.CompilerParams(
            vmem_limit_bytes=VMEM_LIMIT, dimension_semantics=("arbitrary",)
        ),
        cost_estimate=pl.CostEstimate(
            flops=chunk.shape[0] * HALF * 256 * 2 * lanes * 2 * 2,
            bytes_accessed=chunk.size * 4 + math.prod(shape) * 8,
            transcendentals=0,
        ),
    )(codes, counts, chunk, table, turn, held)


def real_transform(real, imag, size):
    if size == 2:
        return [real[0] + real[1], real[0] - real[1]]
    half = size // 2
    quarter = half // 2
    even = real_transform(real[::2], imag[::2], half)
    odd_indices = list(range(1, half, 2))

    def total(terms, a, wave):
        result = None
        for k in odd_indices:
            factor = wave(2.0 * math.pi * k * a / size)
            if abs(factor) < 1e-9:
                continue
            term = terms[k] * factor if abs(factor - 1.0) > 1e-9 else terms[k]
            result = term if result is None else result + term
        return result

    cosines = [total(real, a, math.cos) for a in range(quarter)] + [None]
    sines = [None] + [total(imag, a, math.sin) for a in range(1, quarter + 1)]
    odd = [None] * half
    for a in range(quarter + 1):
        if cosines[a] is None:
            odd[a] = sines[a]
        elif sines[a] is None:
            odd[a] = cosines[a]
        else:
            odd[a] = cosines[a] + sines[a]
            odd[half - a] = sines[a] - cosines[a]
    return [even[a] + odd[a] for a in range(half)] + [even[a] - odd[a] for a in range(half)]


def image_kernel(rows_ref, table_ref, out_ref, mid, *, lanes, scale):
    step = pl.program_id(1)
    tiles = 2 * lanes // 128
    rows = rows_ref.reshape(TILES * tiles * 8, 128)
    take = lambda tile: rows[pl.ds(tile * 8 + step % 8, TILES, tiles * 8), :]
    real = jnp.concatenate([take(tile) for tile in range(tiles // 2)], axis=1)
    imag = jnp.concatenate([take(tile) for tile in range(tiles // 2, tiles)], axis=1)
    data = jnp.concatenate([real, imag], axis=0)
    high = data.astype(jnp.bfloat16)
    low = (data - high.astype(jnp.float32)).astype(jnp.bfloat16)
    dot = lambda left, right: jnp.dot(left, right, preferred_element_type=jnp.float32)
    for part, columns in enumerate((slice(TILES, 3 * TILES), slice(0, 2 * TILES))):
        table_high = table_ref[0, 0, :, columns]
        table_low = table_ref[0, 1, :, columns]
        mid[step, part] = dot(table_high, high) + dot(table_low, high) + dot(table_high, low)

    @pl.when(step == SUB - 1)
    def _():
        place = lambda u: u % 2 * (SUB // 2) + u // 2

        def transform(b_tile, carry):
            where = pl.ds(pl.multiple_of(b_tile * 8, 8), 8)
            for lane in range(lanes // 128):
                at = slice(lane * 128, (lane + 1) * 128)
                take = lambda u, part: mid[place(u), part, where, at]
                real = [take(0, 0)]
                imag = [None]
                for u in range(1, SUB // 2):
                    real.append(take(u, 0) + take(SUB - u, 0))
                    imag.append(take(u, 1) - take(SUB - u, 1))
                real.append(take(SUB // 2, 0))
                imag.append(None)
                for a, value in enumerate(real_transform(real, imag, SUB)):
                    mid[a, 0, where, at] = value * scale
            return carry

        lax.fori_loop(0, TILES // 8, transform, 0)
        wanted = out_ref.shape[1]

        for a in range(SUB):
            out_ref[0, :, a * TILES : (a + 1) * TILES] = mid[a, 0].T[:wanted]


def make_image(rows, table, lanes, wanted, scale):
    def kernel(*refs):
        image_kernel(*refs, lanes=lanes, scale=scale)

    return pl.pallas_call(
        kernel,
        out_shape=jax.ShapeDtypeStruct((2, wanted, G), jnp.float32),
        grid=(2, SUB),
        in_specs=[
            pl.BlockSpec(
                (TILES, 2 * lanes // 128, 8, 128),
                lambda f, i: (0, 0, i // 16 * 4 + f * 2 + i % 16 // 8, 0),
            ),
            pl.BlockSpec((1,) + table.shape[1:], lambda f, i: (i, 0, 0, 0)),
        ],
        out_specs=pl.BlockSpec((1, wanted, G), lambda f, i: (f, 0, 0)),
        scratch_shapes=[pltpu.VMEM((SUB, 2, TILES, lanes), jnp.float32)],
        compiler_params=pltpu.CompilerParams(
            vmem_limit_bytes=VMEM_LIMIT, dimension_semantics=("arbitrary", "arbitrary")
        ),
        cost_estimate=pl.CostEstimate(
            flops=2 * SUB * 3 * 2 * 512 * 512 * lanes,
            bytes_accessed=rows.size * 4 + table.size * 4 + 2 * wanted * G * 4,
            transcendentals=0,
        ),
    )(rows, table)


def local(
    subgrid_pixels,
    tile_offsets,
    station_pairs,
    time_blocks,
    channel_blocks,
    valid_counts,
    aterms,
    channel_weights,
):
    devices = lax.axis_size("row") * lax.axis_size("col")
    slots = subgrid_pixels.shape[0]
    wanted = G // devices
    lanes = max(wanted, 128)
    first_m = (lax.axis_index("row") * lax.axis_size("col") + lax.axis_index("col")) * wanted
    chunks = max(4, slots * devices // 1024)
    per_chunk = slots // chunks

    valid = jnp.arange(slots, dtype=jnp.int32) < valid_counts[0]
    codes = jnp.where(valid, tile_offsets[:, 0] * TILES + tile_offsets[:, 1], 0)
    small = jnp.concatenate([codes, jnp.broadcast_to(valid_counts, (128,))])
    small = lax.all_gather(small, AXES, tiled=True).reshape(devices, slots + 128)
    codes = small[:, :slots].reshape(devices, chunks, per_chunk)
    counts = small[:, slots]

    spectra = spectra_of(
        subgrid_pixels, station_pairs, time_blocks, channel_blocks, valid, aterms, channel_weights
    )
    table, turn = column_tables(first_m, lanes)
    rows = None
    gather = lambda part: lax.all_gather(part, AXES, tiled=True)
    parts = [spectra[chunk * per_chunk : (chunk + 1) * per_chunk] for chunk in range(chunks)]
    got = [gather(part) for part in parts[:IN_FLIGHT]]
    for chunk in range(chunks):
        rows = add_columns(
            got[chunk],
            codes[:, chunk].reshape(-1),
            counts,
            chunk * per_chunk,
            table,
            turn,
            rows,
            lanes,
        )
        if chunk + IN_FLIGHT < chunks:
            part, rows = lax.optimization_barrier((parts[chunk + IN_FLIGHT], rows))
            got.append(gather(part))
    scale = 1.0 / (SUB * math.sqrt(slots * devices))
    return make_image(rows, row_table(), lanes, wanted, scale)


def solution(mesh):
    in_specs = (
        P(AXES, None, None, None),
        P(AXES, None),
        P(AXES, None),
        P(AXES),
        P(AXES),
        P(AXES),
        P(),
        P(),
    )
    out_specs = P(None, AXES, None)
    return jax.shard_map(local, mesh=mesh, in_specs=in_specs, out_specs=out_specs, check_vma=False)
```

```python
import math

import jax
import jax.numpy as jnp
import numpy as np
from jax import lax
from jax.experimental import pallas as pl
from jax.experimental.pallas import tpu as pltpu
from jax.sharding import PartitionSpec as P

G = 8192
SUB = 32
TILES = G // SUB
HALF = 2 * SUB
AXES = ("row", "col")
GROUP = 16
PAD = 8
VMEM_LIMIT = 60 * 1024 * 1024


def split(value):
    high = lax.reduce_precision(value, 8, 7)
    return high.astype(jnp.bfloat16), (value - high).astype(jnp.bfloat16)


def subgrid_table():
    index = np.arange(SUB)
    k = np.arange(SUB // 2)
    u = np.stack([k, np.where(k == 0, SUB // 2, SUB - k)], axis=1)
    turns = (
        index[:, None, None, None, None] * u[None, None, :, :, None]
        + index[None, :, None, None, None] * index[None, None, None, None, :]
    ) % SUB
    wave = np.exp(-2j * np.pi / SUB * turns) / SUB
    table = np.zeros((2, SUB, SUB, SUB // 2, 2, 2, SUB))
    table[0, :, :, :, :, 0] = wave.real
    table[0, :, :, :, :, 1] = wave.imag
    table[1, :, :, :, :, 0] = -wave.imag
    table[1, :, :, :, :, 1] = wave.real
    table = table.reshape(2 * SUB * SUB, 2 * SUB * SUB).astype(np.float32)
    high = table.astype(jnp.bfloat16)
    low = (table - high.astype(np.float32)).astype(jnp.bfloat16)
    return high, low


def spectra_of(pixels, pairs, times, channels, valid, aterms, weights):
    slots = pixels.shape[0]
    first = aterms[pairs[:, 0], times].astype(jnp.float32)
    second = aterms[pairs[:, 1], times].astype(jnp.float32)
    gain_real = first[:, 0] * second[:, 0] + first[:, 1] * second[:, 1]
    gain_imag = first[:, 1] * second[:, 0] - first[:, 0] * second[:, 1]
    matches = channels[:, None] == jnp.arange(weights.shape[0], dtype=jnp.int32)[None, :]
    weight = jnp.sum(jnp.where(matches, weights[None, :], 0.0), axis=1)
    weight = jnp.where(valid, weight, 0.0)[:, None, None]
    real = (pixels[:, 0] * gain_real - pixels[:, 1] * gain_imag) * weight
    imag = (pixels[:, 0] * gain_imag + pixels[:, 1] * gain_real) * weight
    table_high, table_low = subgrid_table()
    dot = lambda left, right: jnp.dot(left, right, preferred_element_type=jnp.float32)
    spectra = []
    for feed in range(2):
        high, low = split(jnp.concatenate([real[:, feed], imag[:, feed]], axis=1))
        out = dot(high, table_high) + dot(low, table_high) + dot(high, table_low)
        spectra.append(out.reshape(slots, SUB // 2, 128))
    return spectra


def phases(turns, modulus):
    angle = (2.0 * math.pi / modulus) * (turns % modulus).astype(jnp.float32)
    return jnp.cos(angle), jnp.sin(angle)


def column_tables(first_m, lanes):
    m = first_m + jnp.arange(lanes, dtype=jnp.int32)
    cos, sin = phases(jnp.arange(SUB, dtype=jnp.int32)[:, None] * m[None, :], G)
    table = jnp.concatenate(
        [jnp.concatenate([cos, -sin], axis=1), jnp.concatenate([sin, cos], axis=1)], axis=0
    )
    high, low = split(table)
    table = jnp.concatenate([high, high, low, jnp.zeros_like(high)], axis=0)
    cos, sin = phases(jnp.arange(TILES, dtype=jnp.int32)[:, None] * m[None, :], TILES)
    return table, jnp.concatenate([cos, -sin], axis=1).reshape(TILES, 2 * lanes // 128, 128)


def row_table():
    b = jnp.arange(TILES, dtype=jnp.int32)
    k = jnp.arange(SUB // 2 + 1, dtype=jnp.int32)
    cos_r, sin_r = phases(b[:, None] * b[None, :], TILES)
    cos_k, sin_k = phases(k[:, None] * b[None, :], G)
    cos = cos_r[None] * cos_k[:, :, None] - sin_r[None] * sin_k[:, :, None]
    sin = sin_r[None] * cos_k[:, :, None] + cos_r[None] * sin_k[:, :, None]
    upper = jnp.concatenate([cos, sin], axis=2)
    lower = jnp.concatenate([-sin, cos], axis=2)
    lower = jnp.concatenate([upper[SUB // 2 :], lower[1 : SUB // 2]], axis=0)
    high, low = split(jnp.concatenate([upper[: SUB // 2], lower], axis=1))
    return jnp.stack([high, low], axis=1)


def feed_kernel(codes, counts, *refs, units, unit_slots, first, last, feed, lanes, wanted, scale):
    arrays = len(units)
    parts = refs[:arrays]
    table_ref, turn_ref, row_ref, held_ref, _, rows_out, image, total, blocks, mid, planes, slab = refs[
        arrays : arrays + 12
    ]
    sem, block_sems, sems = refs[arrays + 12 :]
    step = pl.program_id(0)
    tiles = 2 * lanes // 128
    side_rows = SUB // 2
    is_low = lax.broadcasted_iota(jnp.int32, (GROUP * side_rows, 128), 1) < HALF

    def add_group(unit, start):
        x = blocks[unit % 2, pl.ds(start, GROUP)].reshape(GROUP * side_rows, 128)
        high = x.astype(jnp.bfloat16).astype(jnp.float32)
        low = x - high
        high_turned = pltpu.roll(high, HALF, 1)
        low_turned = pltpu.roll(low, HALF, 1)
        sides = (
            (jnp.where(is_low, high, low_turned), high),
            (jnp.where(is_low, high_turned, low), high_turned),
        )
        left = jnp.concatenate(
            [
                jnp.concatenate([mixed.astype(jnp.bfloat16), other.astype(jnp.bfloat16)], axis=1)
                for mixed, other in sides
            ],
            axis=0,
        )
        mid[...] = jnp.dot(left, table_ref[...], preferred_element_type=jnp.float32)
        for item in range(GROUP):
            code = codes[unit, start + item]
            row = code // TILES
            turns = turn_ref[code % TILES]
            held, added = [], []
            for side, at_row in enumerate((row, TILES - 1 - row)):
                begin = (side * GROUP + item) * side_rows
                for tile in range(tiles // 2):
                    here = slice(tile * 128, (tile + 1) * 128)
                    there = slice(lanes + tile * 128, lanes + (tile + 1) * 128)
                    turn_real = turns[tile : tile + 1]
                    turn_imag = turns[tiles // 2 + tile : tiles // 2 + tile + 1]
                    real = mid[begin : begin + side_rows, here]
                    imag = mid[begin : begin + side_rows, there]
                    new_real = real * turn_real - imag * turn_imag
                    new_imag = real * turn_imag + imag * turn_real
                    for part, new in enumerate((new_real, new_imag if side == 0 else -new_imag)):
                        first_row = (part * (tiles // 2) + tile) * SUB + side * side_rows
                        place = (at_row, slice(first_row, first_row + side_rows))
                        held.append(place)
                        added.append(total[place] + new)
            for place, value in zip(held, added):
                total[place] = value

    def fetch(unit):
        offset = 0
        for part, count in zip(parts, units):
            inside = jnp.logical_and(unit >= offset, unit < offset + count)

            @pl.when(inside)
            def _(part=part, offset=offset):
                pltpu.make_async_copy(
                    part.at[pl.ds((unit - offset) * (unit_slots + 1), unit_slots)],
                    blocks.at[unit % 2],
                    block_sems.at[unit % 2],
                ).start()

            offset += count

    @pl.when(step == 0)
    def _():
        fetch(0)
        if first:
            total[...] = jnp.zeros_like(total)
        else:
            copy = pltpu.make_async_copy(held_ref, total, sem)
            copy.start()
            copy.wait()

        def add_unit(unit, carry):
            @pl.when(unit + 1 < sum(units))
            def _():
                fetch(unit + 1)

            pltpu.make_async_copy(
                parts[0].at[pl.ds(0, unit_slots)], blocks.at[unit % 2], block_sems.at[unit % 2]
            ).wait()

            def one(group, carry):
                add_group(unit, group * GROUP)
                return carry

            lax.fori_loop(0, (counts[unit] + GROUP - 1) // GROUP, one, 0)
            return carry

        lax.fori_loop(0, sum(units), add_unit, 0)

    if not last:

        copy = pltpu.make_async_copy(total, rows_out, sem)
        copy.start()
        copy.wait()
        return

    k = step - 1
    stride = tiles * SUB + PAD
    rows = total.reshape(TILES * stride, 128)

    def take(part, side):
        row = part * (tiles // 2) * SUB + side * side_rows + k
        pieces = [rows[pl.ds(row + tile * SUB, TILES, stride), :] for tile in range(tiles // 2)]
        return jnp.concatenate(pieces, axis=1)

    def transform(data, low_row, high_row):
        high = data.astype(jnp.bfloat16)
        low = (data - high.astype(jnp.float32)).astype(jnp.bfloat16)
        dot = lambda left, right: jnp.dot(left, right, preferred_element_type=jnp.float32)
        table_high = row_ref[0, 0, low_row:high_row]
        table_low = row_ref[0, 1, low_row:high_row]
        return dot(table_high, high) + dot(table_low, high) + dot(table_high, low)

    @pl.when(k == 0)
    def _():
        for side in range(2):
            data = jnp.concatenate([take(0, side), take(1, side)], axis=0)
            planes[side] = transform(data, side * TILES, (side + 1) * TILES)

    @pl.when(k > 0)
    def _():
        data = jnp.concatenate([take(part, 0) + take(part, 1) for part in range(2)], axis=0)
        out = transform(data, 0, 2 * TILES)
        planes[2 * k] = out[:TILES]
        planes[2 * k + 1] = out[TILES:]

    @pl.when(k == SUB // 2 - 1)
    def _():
        def last_stage(b_tile, carry):
            where = pl.ds(pl.multiple_of(b_tile * 8, 8), 8)
            for lane in range(lanes // 128):
                at = slice(lane * 128, (lane + 1) * 128)
                real = [planes[2 * j, where, at] for j in range(SUB // 2)]
                imag = [None] + [planes[2 * j + 1, where, at] for j in range(1, SUB // 2)] + [None]
                real.append(planes[1, where, at])
                for a, value in enumerate(real_transform(real, imag, SUB)):
                    planes[a, where, at] = value * scale
            return carry

        lax.fori_loop(0, TILES // 8, last_stage, 0)
        copies = []
        for a in range(SUB):
            at = slice(a * TILES, (a + 1) * TILES)
            slab[:, at] = planes[a].T[:wanted]
            copies.append(
                pltpu.make_async_copy(slab.at[:, at], image.at[feed, :, at], sems.at[a])
            )
            copies[-1].start()
        for copy in copies:
            copy.wait()


def add_feed(parts, codes, counts, tables, held, image, last, feed, lanes, wanted, scale):
    table, turn, row = tables
    unit_slots = codes.shape[1]
    units = [part.shape[0] // (unit_slots + 1) for part in parts]
    arrays = len(parts)
    shape = (TILES, 2 * lanes // 128 * SUB + PAD, 128)
    first = held is None
    blank = image is None
    if first:
        held = jnp.zeros((8, 128), jnp.float32)
    if blank:
        image = jnp.zeros((8, 128), jnp.float32)
    aliases = {}
    if not first and not last:
        aliases[2 + arrays + 3] = 0
    if not blank:
        aliases[2 + arrays + 4] = 1
    any_spec = pl.BlockSpec(memory_space=pl.ANY)

    def kernel(*refs):
        feed_kernel(
            *refs,
            units=units,
            unit_slots=unit_slots,
            first=first,
            last=last,
            feed=feed,
            lanes=lanes,
            wanted=wanted,
            scale=scale,
        )

    return pl.pallas_call(
        kernel,
        out_shape=[
            jax.ShapeDtypeStruct((8, 128) if last else shape, jnp.float32),
            jax.ShapeDtypeStruct((2, wanted, G), jnp.float32),
        ],
        grid_spec=pltpu.PrefetchScalarGridSpec(
            num_scalar_prefetch=2,
            grid=(1 + (SUB // 2 if last else 0),),
            in_specs=[any_spec] * arrays
            + [
                pl.BlockSpec(table.shape, lambda i, *_: (0, 0)),
                pl.BlockSpec(turn.shape, lambda i, *_: (0, 0, 0)),
                pl.BlockSpec((1,) + row.shape[1:], lambda i, *_: (jnp.maximum(i - 1, 0), 0, 0, 0)),
                any_spec,
                any_spec,
            ],
            out_specs=[any_spec, any_spec],
            scratch_shapes=[
                pltpu.VMEM(shape, jnp.float32),
                pltpu.VMEM((2, unit_slots, SUB // 2, 128), jnp.float32),
                pltpu.VMEM((GROUP * SUB, 2 * lanes), jnp.float32),
                pltpu.VMEM((SUB, TILES, lanes), jnp.float32),
                pltpu.VMEM((wanted, G), jnp.float32),
                pltpu.SemaphoreType.DMA,
                pltpu.SemaphoreType.DMA((2,)),
                pltpu.SemaphoreType.DMA((SUB,)),
            ],
        ),
        input_output_aliases=aliases,
        compiler_params=pltpu.CompilerParams(
            vmem_limit_bytes=VMEM_LIMIT, dimension_semantics=("arbitrary",)
        ),
        cost_estimate=pl.CostEstimate(
            flops=sum(units) * unit_slots * SUB * 256 * 2 * lanes * 2 * 2,
            bytes_accessed=sum(part.size for part in parts) * 4 + math.prod(shape) * 4,
            transcendentals=0,
        ),
    )(codes, counts, *parts, table, turn, row, held, image)


def real_transform(real, imag, size):
    if size == 2:
        return [real[0] + real[1], real[0] - real[1]]
    half = size // 2
    quarter = half // 2
    even = real_transform(real[::2], imag[::2], half)
    odd_indices = list(range(1, half, 2))

    def total(terms, a, wave):
        result = None
        for k in odd_indices:
            factor = wave(2.0 * math.pi * k * a / size)
            if abs(factor) < 1e-9:
                continue
            term = terms[k] * factor if abs(factor - 1.0) > 1e-9 else terms[k]
            result = term if result is None else result + term
        return result

    cosines = [total(real, a, math.cos) for a in range(quarter)] + [None]
    sines = [None] + [total(imag, a, math.sin) for a in range(1, quarter + 1)]
    odd = [None] * half
    for a in range(quarter + 1):
        if cosines[a] is None:
            odd[a] = sines[a]
        elif sines[a] is None:
            odd[a] = cosines[a]
        else:
            odd[a] = cosines[a] + sines[a]
            odd[half - a] = sines[a] - cosines[a]
    return [even[a] + odd[a] for a in range(half)] + [even[a] - odd[a] for a in range(half)]


def local(
    subgrid_pixels,
    tile_offsets,
    station_pairs,
    time_blocks,
    channel_blocks,
    valid_counts,
    aterms,
    channel_weights,
):
    devices = lax.axis_size("row") * lax.axis_size("col")
    slots = subgrid_pixels.shape[0]
    wanted = G // devices
    lanes = max(wanted, 128)
    first_m = (lax.axis_index("row") * lax.axis_size("col") + lax.axis_index("col")) * wanted
    valid = jnp.arange(slots, dtype=jnp.int32) < valid_counts[0]
    codes = jnp.where(valid, tile_offsets[:, 0] * TILES + tile_offsets[:, 1], 0)

    spectra = spectra_of(
        subgrid_pixels, station_pairs, time_blocks, channel_blocks, valid, aterms, channel_weights
    )
    tables = column_tables(first_m, lanes) + (row_table(),)
    scale = 1.0 / (SUB * math.sqrt(slots * devices))

    def gather(feed, start, stop):
        remaining = jnp.clip(valid_counts - start, 0, stop - start)
        details = jnp.concatenate([codes[start:stop], remaining]).astype(jnp.float32)
        details = jnp.pad(details, (0, 128 * SUB // 2 - details.shape[0]))
        details = details.reshape(1, SUB // 2, 128)
        own = jnp.concatenate([spectra[feed][start:stop], details], axis=0)
        return lax.all_gather(own, AXES, tiled=True)

    def add(parts, rows, image, last, feed):
        size = parts[0].shape[0] // devices
        notes = [
            part.reshape(-1, size, SUB // 2, 128)[:, size - 1, 0, :size] for part in parts
        ]
        notes = jnp.concatenate(notes, axis=0).astype(jnp.int32)
        return add_feed(
            parts,
            notes[:, : size - 1],
            notes[:, size - 1],
            tables,
            rows,
            image,
            last,
            feed,
            lanes,
            wanted,
            scale,
        )

    image = None
    if devices <= 32:
        half, late = slots // 2, slots * 3 // 4
        ends = [[(0, half), (half, slots)], [(0, half), (half, late), (late, slots)]]
        pieces = [[gather(feed, *span) for span in spans] for feed, spans in enumerate(ends)]
        for feed in range(2):
            rows = None
            for index, piece in enumerate(pieces[feed]):
                if image is None:
                    piece, tables = lax.optimization_barrier((piece, tables))
                else:
                    piece, image = lax.optimization_barrier((piece, image))
                rows, image = add([piece], rows, image, index == len(pieces[feed]) - 1, feed)
        return image
    size = slots * 32 // devices
    for feed in range(2):
        rows = None
        for start in range(0, slots, size):
            if image is not None:
                spectra[feed], image = lax.optimization_barrier((spectra[feed], image))
            part = gather(feed, start, start + size)
            rows, image = add([part], rows, image, start + size == slots, feed)
    return image


def solution(mesh):
    in_specs = (
        P(AXES, None, None, None),
        P(AXES, None),
        P(AXES, None),
        P(AXES),
        P(AXES),
        P(AXES),
        P(),
        P(),
    )
    out_specs = P(None, AXES, None)
    return jax.shard_map(local, mesh=mesh, in_specs=in_specs, out_specs=out_specs, check_vma=False)
```
